256 devices in a mesh: gx: 16 (over x_hi, z), gy: 16 (over y, x_lo, core).
Axes of the slice: x: 4 (x_hi: 2, x_lo: 2; x = x_hi * 2 + x_lo), y: 4, z: 8, core: 2. Of those that a mesh axis runs over, the one named last changes fastest.
Arguments:
- prediction: float32 [256, 256, 128], P('gx', 'gy'), may hold values from 0 to 1
- label_mask: int32 [256, 256, 128], P('gx', 'gy'), may hold values 0 or 1
- confidence: float32 [256, 256, 128], P('gx', 'gy'), may hold values from 0.5 to 1
Outputs:
- gradient: float32 [256, 256, 128], P('gx', 'gy')
- loss: float32 [], replicated
The draws below stay inside these ranges and needn't reach their ends.
All inputs are finite; a program needn't handle non-finite values. No bound on the sum of `label_mask` on one device may be relied on, other than what follows from the above.
Results may differ from the reference program's by a relative error of at most 0.000025.
Values sent between devices are 32-bit elements; how exact they have to be, the bound alone decides.
No kernel may reach another device: no remote copies, remote signals or barrier semaphores. Data moves between devices by JAX's collectives and lax.ppermute only.
A program may use at most 128 MiB of HBM per device.

```python
from functools import partial
import jax
import jax.numpy as jnp
from jax import lax

NZ = 128
ITERS = 3
NX = 256
NY = 256


def place_ends(drawn, stream_key, smallest, top_value):
    dims = drawn.shape
    place = [jax.random.randint(jax.random.fold_in(stream_key, axis), (), 0, dims[axis]) for axis in range(len(dims))]
    drawn = drawn.at[tuple(place)].set(smallest)
    longest = dims.index(max(dims))
    place[longest] = (place[longest] + 1) % dims[longest]
    return drawn.at[tuple(place)].set(top_value)


def block_scale(stream_key, dims, shards, low, high):
    factor_of, own = 1.0, jax.random.fold_in(stream_key, 6)
    for position, parts in shards:
        draws = jnp.exp(jax.random.uniform(jax.random.fold_in(own, position), (parts,), jnp.float32, low / len(shards), high / len(shards)))
        factor_of = factor_of * jnp.repeat(draws, dims[position] // parts).reshape([-1 if axis == position else 1 for axis in range(len(dims))])
    return factor_of


def setup_inputs(seed: int = 0) -> dict:
    seeds = jax.random.split(jax.random.key(seed), 4)
    prediction = jnp.clip(1.0 * jax.random.uniform(seeds[0], (NX, NY, NZ), jnp.float32) ** block_scale(seeds[0], (NX, NY, NZ), ((0, 16), (1, 16)), -0.2, 0.2), 0.0, 1.0)
    label_mask = place_ends((jax.random.randint(seeds[1], (NX, NY, NZ), 0, 2) < 1).astype(jnp.int32), jax.random.fold_in(seeds[1], 1), 0, 1)
    confidence = jnp.clip(0.5 + 0.5 * jax.random.uniform(seeds[2], (NX, NY, NZ), jnp.float32) ** block_scale(seeds[2], (NX, NY, NZ), ((0, 16), (1, 16)), -0.2, 0.2), 0.5, 1.0)
    return {"prediction": prediction, "label_mask": label_mask, "confidence": confidence}


def sides(volume, axis, first, last):
    widths = [(0, 0), (0, 0), (0, 0)]
    widths[axis] = (1, 1)
    padded = jnp.pad(volume, widths, mode='edge')
    length = volume.shape[axis]
    lower = lax.slice_in_dim(padded, 0, length, axis=axis)
    upper = lax.slice_in_dim(padded, 2, length + 2, axis=axis)
    if first is not None:
        lower = jnp.where(first, volume, lower)
        upper = jnp.where(last, volume, upper)
    return (lower, upper)

def pooled(volume, axis, first, last, picker):
    lower, upper = sides(volume, axis, first, last)
    return picker(picker(lower, volume), upper)

def erode(volume, edges):
    along_one = pooled(volume, 0, edges[0], edges[1], jnp.minimum)
    along_two = pooled(volume, 1, edges[2], edges[3], jnp.minimum)
    along_three = pooled(volume, 2, None, None, jnp.minimum)
    return jnp.minimum(jnp.minimum(along_one, along_two), along_three)

def dilate(volume, edges):
    result = pooled(volume, 0, edges[0], edges[1], jnp.maximum)
    result = pooled(result, 1, edges[2], edges[3], jnp.maximum)
    return pooled(result, 2, None, None, jnp.maximum)

def skel_step(state, edges):
    volume, skeleton_sum = state
    eroded = erode(volume, edges)
    delta = jax.nn.relu(volume - dilate(eroded, edges))
    skeleton_sum = skeleton_sum + jax.nn.relu(delta - skeleton_sum * delta)
    return (eroded, skeleton_sum)

def skeleton(volume, edges):
    eroded = erode(volume, edges)
    skeleton_sum = jax.nn.relu(volume - dilate(eroded, edges))
    state = (eroded, skeleton_sum)
    stepper = jax.checkpoint(partial(skel_step, edges=edges))
    for index in range(ITERS):
        state = stepper(state)
    return state[1]

def reference(prediction, label_mask, confidence):
    edges = (None, None, None, None)
    target = label_mask.astype(jnp.float32) * confidence
    skel_pred, pullback = jax.vjp(lambda volume: skeleton(volume, edges), prediction)
    skel_target = skeleton(target, edges)
    sum_a = jnp.sum(skel_pred * target)
    sum_b = jnp.sum(skel_pred)
    sum_c = jnp.sum(skel_target * prediction)
    sum_d = jnp.sum(skel_target)
    precision = (sum_a + 1.0) / (sum_b + 1.0)
    sensitivity = (sum_c + 1.0) / (sum_d + 1.0)
    together = precision + sensitivity
    loss = 1.0 - 2.0 * precision * sensitivity / together
    cells = jnp.float32(NX * NY * NZ)
    coef_pred = cells * (-2.0 * sensitivity * sensitivity / (together * together)) / (sum_b + 1.0)
    coef_target = cells * (-2.0 * precision * precision / (together * together)) / (sum_d + 1.0)
    cotangent = coef_pred * (target - precision)
    gradient = pullback(cotangent)[0] + coef_target * skel_target
    return (gradient, loss)
```

```python
import jax
import jax.numpy as jnp
from jax import lax
from jax.experimental import pallas as pl
from jax.experimental.pallas import tpu as pltpu
from jax.sharding import PartitionSpec as P

ITERS = 3
OWN = 16
WIDE = 10
NEAR = 5
YP = 40
Y0 = 12
XP = 40
HIGH, LOW = 36, 37
PLANE = XP * YP
LV = 32
DENSE = XP * LV
INF = float("inf")


def lanes():
    return lax.broadcasted_iota(jnp.int32, (8, 128), 1)


def sublanes():
    return lax.broadcasted_iota(jnp.int32, (8, 128), 0)


class Axes:
    def __init__(self, nb):
        size_x, size_y = lax.axis_size("gx"), lax.axis_size("gy")
        gx, gy = lax.axis_index("gx"), lax.axis_index("gy")
        self.first_x, self.last_x = gx == 0, gx == size_x - 1
        self.first_y, self.last_y = gy == 0, gy == size_y - 1
        self.nb = nb
        start = 0 if nb == 5 else 4
        self.low_s, self.low_b = divmod(Y0 - start, nb)
        self.up_s, self.up_b = divmod(Y0 + OWN - 1 - start, nb)
        sub, lane = sublanes(), lanes()
        self.low_y = (sub == self.low_s) & self.first_y
        self.up_y = (sub == self.up_s) & self.last_y
        self.low_z, self.up_z = lane == 0, lane == 127
        self.q_y = jnp.where(self.up_y, 0.25, 0.5)
        self.q_z = jnp.where(self.up_z, 0.25, 0.5)

    def rows(self, x, stand_in):
        below = jnp.where((x == WIDE) & self.first_x, stand_in, x - 1)
        above = jnp.where((x == WIDE + OWN - 1) & self.last_x, stand_in, x + 1)
        return below, above

    def q_x(self, x):
        return jnp.where((x == WIDE + OWN - 1) & self.last_x, 0.25, 0.5)

    def along_y(self, v, fill):
        nb = self.nb
        lower = [pltpu.roll(v[nb - 1], 1, 0)] + v[: nb - 1]
        upper = v[1:] + [pltpu.roll(v[0], 7, 0)]
        lower[self.low_b] = jnp.where(self.low_y, fill, lower[self.low_b])
        upper[self.up_b] = jnp.where(self.up_y, fill, upper[self.up_b])
        return lower, upper

    def along_z(self, v, fill):
        lower = [jnp.where(self.low_z, fill, pltpu.roll(a, 1, 1)) for a in v]
        upper = [jnp.where(self.up_z, fill, pltpu.roll(a, 127, 1)) for a in v]
        return lower, upper

    def back_y(self, gl, gu):
        nb = self.nb
        from_above = gl[1:] + [pltpu.roll(gl[0], 7, 0)]
        from_below = [pltpu.roll(gu[nb - 1], 1, 0)] + gu[: nb - 1]
        return [a + b for a, b in zip(from_above, from_below)]


def back_z(gl, gu):
    return [pltpu.roll(a, 127, 1) + pltpu.roll(b, 1, 1) for a, b in zip(gl, gu)]


def load(ref, base, x, nb):
    start = 0 if nb == 5 else 4
    return [ref[pl.ds(base + x * YP + start + b, 8, stride=nb), :] for b in range(nb)]


def store(ref, base, x, nb, v):
    start = 0 if nb == 5 else 4
    for b in range(nb):
        ref[pl.ds(base + x * YP + start + b, 8, stride=nb), :] = v[b]


def load_dense(ref, base, x):
    return [ref[pl.ds(pl.multiple_of(base + x * LV + 8 * b, 8), 8), :] for b in range(4)]


def store_dense(ref, base, x, v):
    for b in range(4):
        ref[pl.ds(pl.multiple_of(base + x * LV + 8 * b, 8), 8), :] = v[b]


def each(pick, *lists):
    out = lists[0]
    for other in lists[1:]:
        out = [pick(a, b) for a, b in zip(out, other)]
    return out


def pack_rows_kernel(pred, label, conf, target, send_a, send_b):
    even = lax.rem(lax.axis_index("gx"), 2) == 0
    target[...] = label[...].astype(jnp.float32) * conf[...]
    wide, near = WIDE * OWN, NEAR * OWN
    total = OWN * OWN
    for ref, last in ((send_a, even), (send_b, jnp.logical_not(even))):
        from_pred = pl.multiple_of(jnp.where(last, total - wide, 0), 8)
        from_target = pl.multiple_of(jnp.where(last, total - near, 0), 8)
        ref[0:wide, :] = pred[pl.ds(from_pred, wide), :]
        ref[wide : wide + near, :] = target[pl.ds(from_target, near), :]


XB, TB = 5, 4
SEND = (WIDE * XB + NEAR * TB) * 8


def pack_columns_kernel(pred, target, rows_a, rows_b, send_a, send_b, wide_pred, wide_target):
    even = lax.rem(lax.axis_index("gx"), 2) == 0
    wide, near, total = WIDE * OWN, NEAR * OWN, OWN * OWN
    wide_pred[wide : wide + total, :] = pred[...]
    wide_target[near : near + total, :] = target[...]
    for ref, after in ((rows_a, even), (rows_b, jnp.logical_not(even))):
        to_pred = pl.multiple_of(jnp.where(after, wide + total, 0), 8)
        to_target = pl.multiple_of(jnp.where(after, near + total, 0), 8)
        wide_pred[pl.ds(to_pred, wide), :] = ref[0:wide, :]
        wide_target[pl.ds(to_target, near), :] = ref[wide : wide + near, :]
    even = lax.rem(lax.axis_index("gy"), 2) == 0
    for ref, last in ((send_a, even), (send_b, jnp.logical_not(even))):
        start = jnp.where(last, OWN - WIDE, 0)
        for j in range(WIDE):
            for i in range(XB):
                ref[pl.ds((j * XB + i) * 8, 8), :] = wide_pred[pl.ds(i * 128 + start + j, 8, stride=OWN), :]
        start = jnp.where(last, OWN - NEAR, 0)
        for j in range(NEAR):
            for i in range(TB):
                ref[pl.ds((WIDE * XB + j * TB + i) * 8, 8), :] = wide_target[
                    pl.ds(i * 128 + start + j, 8, stride=OWN), :
                ]


def unpack(pred, target, rows_a, rows_b, cols_a, cols_b, vol, tvol):
    even = lax.rem(lax.axis_index("gx"), 2) == 0
    wide = WIDE * OWN

    def whole(i, _):
        own = pl.ds(pl.multiple_of(i * OWN, OWN), OWN)
        vol[pl.ds((WIDE + i) * YP + Y0, OWN), :] = pred[own, :]
        tvol[pl.ds((WIDE + i) * YP + Y0, OWN), :] = target[own, :]
        return 0

    lax.fori_loop(0, OWN, whole, 0)
    for ref, after in ((rows_a, even), (rows_b, jnp.logical_not(even))):
        to_pred = jnp.where(after, WIDE + OWN, 0)
        to_target = jnp.where(after, WIDE + OWN, WIDE - NEAR)

        def one(i, _, ref=ref, to_pred=to_pred):
            vol[pl.ds((to_pred + i) * YP + Y0, OWN), :] = ref[pl.ds(pl.multiple_of(i * OWN, OWN), OWN), :]
            return 0

        lax.fori_loop(0, WIDE, one, 0)

        def two(i, _, ref=ref, to_target=to_target):
            tvol[pl.ds((to_target + i) * YP + Y0, OWN), :] = ref[pl.ds(pl.multiple_of(wide + i * OWN, OWN), OWN), :]
            return 0

        lax.fori_loop(0, NEAR, two, 0)
    even = lax.rem(lax.axis_index("gy"), 2) == 0
    for ref, after in ((cols_a, even), (cols_b, jnp.logical_not(even))):
        y = jnp.where(after, Y0 + OWN, Y0 - WIDE)
        for j in range(WIDE):
            for i in range(XB):
                vol[pl.ds(i * 8 * YP + y + j, 8, stride=YP), :] = ref[pl.ds((j * XB + i) * 8, 8), :]
        y = jnp.where(after, Y0 + OWN, Y0 - NEAR)
        for j in range(NEAR):
            for i in range(TB):
                tvol[pl.ds((NEAR + i * 8) * YP + y + j, 8, stride=YP), :] = ref[
                    pl.ds((WIDE * XB + j * TB + i) * 8, 8), :
                ]
    for ref in (vol, tvol):
        for k in range(ITERS + 2):
            ref[pl.ds(k * PLANE + HIGH * YP, YP), :] = jnp.full((YP, 128), INF, jnp.float32)
            ref[pl.ds(k * PLANE + LOW * YP, YP), :] = jnp.full((YP, 128), -INF, jnp.float32)


def erode_rows(vol, k, first, last, axes):
    nb = axes.nb
    base = k * PLANE

    def row(x, _):
        below, above = axes.rows(x, HIGH)
        v = load(vol, base, x, nb)
        low, up = load(vol, base, below, nb), load(vol, base, above, nb)
        m = each(jnp.minimum, v, low, up, *axes.along_y(v, INF), *axes.along_z(v, INF))
        store(vol, base + PLANE, x, nb, m)
        return 0

    lax.fori_loop(first, last, row, 0)


def dilated(vol, base, x, axes):
    below, above = axes.rows(x, LOW)
    e = load(vol, base, x, 4)
    a = each(jnp.maximum, e, load(vol, base, below, 4), load(vol, base, above, 4))
    b = each(jnp.maximum, a, *axes.along_y(a, -INF))
    return each(jnp.maximum, b, *axes.along_z(b, -INF))


def skeleton_rows(vol, k, first, last, axes, skel, delta_ref):
    base = k * PLANE

    def row(x, _):
        d = dilated(vol, base + PLANE, x, axes)
        v = load(vol, base, x, 4)
        s = load_dense(skel, k * DENSE, x)
        delta = [jnp.maximum(a - b, 0.0) for a, b in zip(v, d)]
        if delta_ref is not None:
            store_dense(delta_ref, k * DENSE, x, delta)
        s = [a + jnp.maximum(b - a * b, 0.0) for a, b in zip(s, delta)]
        store_dense(skel, (k + 1) * DENSE, x, s)
        return 0

    lax.fori_loop(first, last, row, 0)


def forward_kernel(
    pred, target, rows_a, rows_b, cols_a, cols_b, vol, skel, delta, cot, skel_target, sums, tvol, tskel
):
    unpack(pred, target, rows_a, rows_b, cols_a, cols_b, vol, tvol)
    skel[0:DENSE, :] = jnp.zeros((DENSE, 128), jnp.float32)
    tskel[0:DENSE, :] = jnp.zeros((DENSE, 128), jnp.float32)
    five, four = Axes(5), Axes(4)
    near = WIDE - NEAR
    end = WIDE + OWN + NEAR

    def step(k, _):
        erode_rows(vol, k, 1 + k, 35 - k, five)
        erode_rows(tvol, k, near + 1 + k, end - 1 - k, four)
        skeleton_rows(vol, k, near, end, four, skel, delta)
        skeleton_rows(tvol, k, WIDE, WIDE + OWN, four, tskel, None)
        return 0

    lax.fori_loop(0, ITERS + 1, step, 0)
    sub = sublanes()
    own_y = (sub >= 2) & (sub < 6)
    inside_y = jnp.logical_not(((sub < 2) & four.first_y) | ((sub >= 6) & four.last_y))
    done = (ITERS + 1) * DENSE
    zero = jnp.zeros((8, 128), jnp.float32)

    def total(x, acc):
        sp, st = load_dense(skel, done, x), load_dense(tskel, done, x)
        p, t = load(vol, 0, x, 4), load(tvol, 0, x, 4)
        a = acc[0] + sum(u * w for u, w in zip(sp, t))
        c = acc[2] + sum(u * w for u, w in zip(st, p))
        store_dense(skel_target, 0, x - WIDE, st)
        return a, acc[1] + sum(sp), c, acc[3] + sum(st)

    acc = lax.fori_loop(WIDE, WIDE + OWN, total, (zero,) * 4)
    lane = lax.broadcasted_iota(jnp.int32, (8, 128), 1)
    row = jnp.zeros((8, 128), jnp.float32)
    for i in range(4):
        row = jnp.where(lane == i, jnp.sum(jnp.where(own_y, acc[i], 0.0)), row)
    for i in range(sums.shape[0] // 8):
        sums[i * 8 : i * 8 + 8, :] = row

    def start(x, _):
        outside = ((x < WIDE) & four.first_x) | ((x >= WIDE + OWN) & four.last_x)
        keep = inside_y & jnp.logical_not(outside)
        t = load(tvol, 0, x, 4)
        store_dense(cot, 0, x, [jnp.where(keep, a, 0.0) for a in t])
        store_dense(cot, DENSE, x, [jnp.where(keep, 1.0, 0.0)] * 4)
        return 0

    lax.fori_loop(near, end, start, 0)


def split_weight(v, other, tie):
    return jnp.where(v > other, 0.0, jnp.where(v == other, tie, 1.0))


def split_weight_min(v, other, tie):
    return jnp.where(v < other, 0.0, jnp.where(v == other, tie, 1.0))


def pool_weights(v, low, up, q, minimum):
    pick, weight = (jnp.minimum, split_weight_min) if minimum else (jnp.maximum, split_weight)
    t = pick(low, v)
    to_up = weight(t, up, 0.5)
    to_low = weight(v, low, q)
    return to_low * (1.0 - to_up), to_up, pick(t, up)


def backward_kernel(vol, skel, delta, cot, grad_t, grad_1, gs, ga, gd):
    axes = Axes(4)
    near, end = WIDE - NEAR, WIDE + OWN + NEAR
    gs[...] = cot[...]
    ga[...] = jnp.zeros((2 * DENSE, 128), jnp.float32)
    zeros = [jnp.zeros((8, 128), jnp.float32)] * 4
    pair = (0, DENSE)

    def step(i, _):
        k = ITERS - i
        base = k * PLANE

        def undilate(x, carry):
            below, above = axes.rows(x, LOW)
            e = load(vol, base + PLANE, x, 4)
            low_x, up_x = load(vol, base + PLANE, below, 4), load(vol, base + PLANE, above, 4)
            q_x = axes.q_x(x)
            d, s = load_dense(delta, k * DENSE, x), load_dense(skel, k * DENSE, x)
            wx = [pool_weights(a, b, c, q_x, False) for a, b, c in zip(e, low_x, up_x)]
            a = [w[2] for w in wx]
            low, up = axes.along_y(a, -INF)
            wy = [pool_weights(a[j], low[j], up[j], axes.q_y if j == axes.up_b else 0.5, False) for j in range(4)]
            b = [w[2] for w in wy]
            low, up = axes.along_z(b, -INF)
            wz = [pool_weights(b[j], low[j], up[j], axes.q_z, False) for j in range(4)]
            out = []
            for c, at in enumerate(pair):
                pending, ahead = carry[c]
                g = load_dense(gs, at, x)
                kept = [jnp.where(u - v * u > 0.0, w, 0.0) for u, v, w in zip(d, s, g)]
                store_dense(gs, at, x, [w - m * u for u, m, w in zip(d, kept, g)])
                g = [jnp.where(u > 0.0, m * (1.0 - v), 0.0) for u, v, m in zip(d, s, kept)]
                store_dense(gd, at, x, g)
                gl, gu = [h * w[0] for h, w in zip(g, wz)], [h * w[1] for h, w in zip(g, wz)]
                g = [h - m - n + o for h, m, n, o in zip(g, gl, gu, back_z(gl, gu))]
                gl, gu = [h * w[0] for h, w in zip(g, wy)], [h * w[1] for h, w in zip(g, wy)]
                g = [h - m - n + o for h, m, n, o in zip(g, gl, gu, axes.back_y(gl, gu))]
                gl, gu = [h * w[0] for h, w in zip(g, wx)], [h * w[1] for h, w in zip(g, wx)]
                g = [h - m - n + o for h, m, n, o in zip(g, gl, gu, ahead)]
                old = load_dense(ga, at, x - 1)
                store_dense(ga, at, x - 1, [h - m - n for h, m, n in zip(old, pending, gl)])
                out.append((g, gu))
            return out

        lax.fori_loop(8 - k, 28 + k, undilate, [(zeros, zeros)] * 2)

        def unerode(x, carry):
            below, above = axes.rows(x, HIGH)
            v = load(vol, base, x, 4)
            low_x, up_x = load(vol, base, below, 4), load(vol, base, above, 4)
            q_x = axes.q_x(x)
            wx = [pool_weights(a, b, c, q_x, True) for a, b, c in zip(v, low_x, up_x)]
            low, up = axes.along_y(v, INF)
            wy = [pool_weights(v[j], low[j], up[j], axes.q_y if j == axes.up_b else 0.5, True) for j in range(4)]
            low, up = axes.along_z(v, INF)
            wz = [pool_weights(v[j], low[j], up[j], axes.q_z, True) for j in range(4)]
            share = []
            for j in range(4):
                one, two, three = wx[j][2], wy[j][2], wz[j][2]
                to_three = split_weight_min(jnp.minimum(one, two), three, 0.5)
                rest = 1.0 - to_three
                to_two = split_weight_min(one, two, 0.5) * rest
                to_one = rest - to_two
                share.append(
                    (to_one * wx[j][0], to_one * wx[j][1], to_two * wy[j][0], to_two * wy[j][1],
                     to_three * wz[j][0], to_three * wz[j][1])
                )
            out = []
            for c, at in enumerate(pair):
                pending, ahead = carry[c]
                g = load_dense(ga, at, x)
                parts = [[h * w[n] for h, w in zip(g, share)] for n in range(6)]
                for part in parts:
                    g = [h - m for h, m in zip(g, part)]
                g = each(jnp.add, g, axes.back_y(parts[2], parts[3]), back_z(parts[4], parts[5]), ahead)
                direct = load_dense(gd, at, x - 1)
                store_dense(ga, at, x - 1, each(jnp.add, direct, pending, parts[0]))
                out.append((g, parts[1]))
            return out

        lax.fori_loop(9 - k, 27 + k, unerode, [(zeros, zeros)] * 2)
        return 0

    lax.fori_loop(0, ITERS + 1, step, 0)
    own = pl.ds(WIDE * LV, OWN * LV)
    grad_t[...] = ga[own, :]
    grad_1[...] = ga[pl.ds(DENSE + WIDE * LV, OWN * LV), :]


def finish_kernel(cells, sums, grad_t, grad_1, skel_target, gradient, loss, natural):
    total = jnp.zeros((8, 128), jnp.float32)
    for i in range(sums.shape[0] // 8):
        total = total + sums[i * 8 : i * 8 + 8, :]
    lane = lanes()
    sum_a, sum_b, sum_c, sum_d = (
        jnp.broadcast_to(jnp.sum(jnp.where(lane == i, total, 0.0)), (8, 128)) for i in range(4)
    )
    precision = (sum_a + 1.0) / (sum_b + 1.0)
    sensitivity = (sum_c + 1.0) / (sum_d + 1.0)
    together = precision + sensitivity
    loss[...] = 1.0 - 2.0 * precision * sensitivity / together
    coef_pred = cells * (-2.0 * sensitivity * sensitivity / (together * together)) / (sum_b + 1.0)
    coef_target = cells * (-2.0 * precision * precision / (together * together)) / (sum_d + 1.0)

    def row(x, _):
        t, one, s = load_dense(grad_t, 0, x), load_dense(grad_1, 0, x), load_dense(skel_target, 0, x)
        for b in range(4):
            natural[pl.ds(x * LV + b, 8, stride=4), :] = (
                coef_pred * (t[b] - precision * one[b]) + coef_target * s[b]
            )
        return 0

    lax.fori_loop(0, OWN, row, 0)
    for x in range(OWN):
        gradient[x * OWN : (x + 1) * OWN, :] = natural[x * LV + 8 : x * LV + 24, :]


def call(kernel, out, scratch=(), cost=None):
    vmem = pl.BlockSpec(memory_space=pltpu.VMEM)

    def run(*args):
        return pl.pallas_call(
            kernel,
            out_shape=[jax.ShapeDtypeStruct(s, jnp.float32) for s in out],
            in_specs=[vmem] * len(args),
            out_specs=[vmem] * len(out),
            scratch_shapes=[pltpu.VMEM(s, jnp.float32) for s in scratch],
            compiler_params=pltpu.CompilerParams(vmem_limit_bytes=12 * 2**20),
            cost_estimate=cost,
        )(*args)

    return run


def swapped(value, axis, shift):
    size = lax.axis_size(axis)
    pairs = [((i + shift) % size, ((i ^ 1) + shift) % size) for i in range(size)]
    return lax.ppermute(value, axis, pairs)


def body(prediction, label_mask, confidence):
    rows, cols, planes = prediction.shape
    flat = (rows * cols, planes)
    devices = lax.axis_size("gx") * lax.axis_size("gy")
    cells = float(devices * rows * cols * planes)
    pred = prediction.reshape(flat)
    side = ((WIDE + NEAR) * OWN, 128)
    target, send_a, send_b = call(pack_rows_kernel, [flat, side, side])(
        pred, label_mask.reshape(flat), confidence.reshape(flat)
    )
    rows_a, rows_b = swapped(send_a, "gx", 0), swapped(send_b, "gx", 1)
    side = (SEND, 128)
    send_a, send_b = call(
        pack_columns_kernel, [side, side], [(XB * 8 * OWN, 128), (TB * 8 * OWN, 128)]
    )(pred, target, rows_a, rows_b)
    cols_a, cols_b = swapped(send_a, "gy", 0), swapped(send_b, "gy", 1)
    levels = ITERS + 2
    vol, skel, delta, cot, skel_target, sums = call(
        forward_kernel,
        [(levels * PLANE, 128), (levels * DENSE, 128), ((ITERS + 1) * DENSE, 128), (2 * DENSE, 128), (OWN * LV, 128), (devices, 128)],
        [(levels * PLANE, 128), (levels * DENSE, 128)],
    )(pred, target, rows_a, rows_b, cols_a, cols_b)
    sums = lax.all_to_all(sums.reshape(devices, 1, 128), ("gx", "gy"), 0, 0).reshape(devices, 128)
    grad_t, grad_1 = call(
        backward_kernel,
        [(OWN * LV, 128)] * 2,
        [(2 * DENSE, 128)] * 3,
        pl.CostEstimate(flops=100_000_000, bytes_accessed=20_000_000, transcendentals=0),
    )(vol, skel, delta, cot)

    def finish(*refs):
        finish_kernel(jnp.float32(cells), *refs)

    gradient, loss = call(finish, [flat, (8, 128)], [(OWN * LV, 128)])(sums, grad_t, grad_1, skel_target)
    return gradient.reshape(rows, cols, planes), loss[0, 0]


def solution(mesh):
    placed = (P("gx", "gy", None), P("gx", "gy", None), P("gx", "gy", None))
    return jax.shard_map(
        body, mesh=mesh, in_specs=placed, out_specs=(P("gx", "gy", None), P()), check_vma=False
    )
```

```python
import jax
import jax.numpy as jnp
from jax import lax
from jax.experimental import pallas as pl
from jax.experimental.pallas import tpu as pltpu
from jax.sharding import PartitionSpec as P

ITERS = 3
RE, RD, RU, RV = 4, 4, 4, 4
OWN = 16
WIDE = 10
NEAR = 5
YP = 40
Y0 = 12
XP = 40
HIGH, LOW = 2.0, -1.0
PLANE = XP * YP
LV = 32
DENSE = XP * LV


def lanes():
    return lax.broadcasted_iota(jnp.int32, (8, 128), 1)


def sublanes():
    return lax.broadcasted_iota(jnp.int32, (8, 128), 0)


class Axes:
    def __init__(self, nb):
        size_x, size_y = lax.axis_size("gx"), lax.axis_size("gy")
        gx, gy = lax.axis_index("gx"), lax.axis_index("gy")
        self.first_x, self.last_x = gx == 0, gx == size_x - 1
        self.first_y, self.last_y = gy == 0, gy == size_y - 1
        self.nb = nb
        start = 0 if nb == 5 else 4
        self.low_s, self.low_b = divmod(Y0 - start, nb)
        self.up_s, self.up_b = divmod(Y0 + OWN - 1 - start, nb)
        sub, lane = sublanes(), lanes()
        self.low_y = (sub == self.low_s) & self.first_y
        self.up_y = (sub == self.up_s) & self.last_y
        self.low_z, self.up_z = lane == 0, lane == 127
        self.q_y = jnp.where(self.up_y, 0.25, 0.5)
        self.q_z = jnp.where(self.up_z, 0.25, 0.5)

    def fence(self, ref, base, value):
        for face, x in ((self.first_x, WIDE - 1), (self.last_x, WIDE + OWN)):

            @pl.when(face)
            def _(x=x):
                ref[pl.ds(pl.multiple_of(base + x * YP, 8), YP), :] = jnp.full((YP, 128), value, jnp.float32)

    def q_x(self, x):
        return jnp.where((x == WIDE + OWN - 1) & self.last_x, 0.25, 0.5)

    def along_y(self, v, fill):
        nb = self.nb
        lower = [pltpu.roll(v[nb - 1], 1, 0)] + v[: nb - 1]
        upper = v[1:] + [pltpu.roll(v[0], 7, 0)]
        lower[self.low_b] = jnp.where(self.low_y, fill, lower[self.low_b])
        upper[self.up_b] = jnp.where(self.up_y, fill, upper[self.up_b])
        return lower, upper

    def along_z(self, v, fill):
        lower = [jnp.where(self.low_z, fill, pltpu.roll(a, 1, 1)) for a in v]
        upper = [jnp.where(self.up_z, fill, pltpu.roll(a, 127, 1)) for a in v]
        return lower, upper

    def back_y(self, gl, gu):
        nb = self.nb
        from_above = gl[1:] + [pltpu.roll(gl[0], 7, 0)]
        from_below = [pltpu.roll(gu[nb - 1], 1, 0)] + gu[: nb - 1]
        return [a + b for a, b in zip(from_above, from_below)]


def back_z(gl, gu):
    return [pltpu.roll(a, 127, 1) + pltpu.roll(b, 1, 1) for a, b in zip(gl, gu)]


def load(ref, base, x, nb):
    start = 0 if nb == 5 else 4
    return [ref[pl.ds(base + x * YP + start + b, 8, stride=nb), :] for b in range(nb)]


def store(ref, base, x, nb, v):
    start = 0 if nb == 5 else 4
    for b in range(nb):
        ref[pl.ds(base + x * YP + start + b, 8, stride=nb), :] = v[b]


def load_dense(ref, base, x):
    return [ref[pl.ds(pl.multiple_of(base + x * LV + 8 * b, 8), 8), :] for b in range(4)]


def store_dense(ref, base, x, v):
    for b in range(4):
        ref[pl.ds(pl.multiple_of(base + x * LV + 8 * b, 8), 8), :] = v[b]


def each(pick, *lists):
    out = lists[0]
    for other in lists[1:]:
        out = [pick(a, b) for a, b in zip(out, other)]
    return out


def pack_rows_kernel(pred, label, conf, target, send_a, send_b):
    even = lax.rem(lax.axis_index("gx"), 2) == 0
    target[...] = label[...].astype(jnp.float32) * conf[...]
    wide, near = WIDE * OWN, NEAR * OWN
    total = OWN * OWN
    for ref, last in ((send_a, even), (send_b, jnp.logical_not(even))):
        from_pred = pl.multiple_of(jnp.where(last, total - wide, 0), 8)
        from_target = pl.multiple_of(jnp.where(last, total - near, 0), 8)
        ref[0:wide, :] = pred[pl.ds(from_pred, wide), :]
        ref[wide : wide + near, :] = target[pl.ds(from_target, near), :]


XB, TB = 5, 4
SEND = (WIDE * XB + NEAR * TB) * 8


def pack_columns_kernel(pred, target, rows_a, rows_b, send_a, send_b, wide_pred, wide_target):
    even = lax.rem(lax.axis_index("gx"), 2) == 0
    wide, near, total = WIDE * OWN, NEAR * OWN, OWN * OWN
    wide_pred[wide : wide + total, :] = pred[...]
    wide_target[near : near + total, :] = target[...]
    for ref, after in ((rows_a, even), (rows_b, jnp.logical_not(even))):
        to_pred = pl.multiple_of(jnp.where(after, wide + total, 0), 8)
        to_target = pl.multiple_of(jnp.where(after, near + total, 0), 8)
        wide_pred[pl.ds(to_pred, wide), :] = ref[0:wide, :]
        wide_target[pl.ds(to_target, near), :] = ref[wide : wide + near, :]
    even = lax.rem(lax.axis_index("gy"), 2) == 0
    for ref, last in ((send_a, even), (send_b, jnp.logical_not(even))):
        start = jnp.where(last, OWN - WIDE, 0)
        for j in range(WIDE):
            for i in range(XB):
                ref[pl.ds((j * XB + i) * 8, 8), :] = wide_pred[pl.ds(i * 128 + start + j, 8, stride=OWN), :]
        start = jnp.where(last, OWN - NEAR, 0)
        for j in range(NEAR):
            for i in range(TB):
                ref[pl.ds((WIDE * XB + j * TB + i) * 8, 8), :] = wide_target[
                    pl.ds(i * 128 + start + j, 8, stride=OWN), :
                ]


def unpack(pred, target, rows_a, rows_b, cols_a, cols_b, vol, tvol):
    even = lax.rem(lax.axis_index("gx"), 2) == 0
    wide = WIDE * OWN

    def whole(i, _):
        own = pl.ds(pl.multiple_of(i * OWN, OWN), OWN)
        vol[pl.ds((WIDE + i) * YP + Y0, OWN), :] = pred[own, :]
        tvol[pl.ds((WIDE + i) * YP + Y0, OWN), :] = target[own, :]
        return 0

    lax.fori_loop(0, OWN, whole, 0)
    for ref, after in ((rows_a, even), (rows_b, jnp.logical_not(even))):
        to_pred = jnp.where(after, WIDE + OWN, 0)
        to_target = jnp.where(after, WIDE + OWN, WIDE - NEAR)

        def one(i, _, ref=ref, to_pred=to_pred):
            vol[pl.ds((to_pred + i) * YP + Y0, OWN), :] = ref[pl.ds(pl.multiple_of(i * OWN, OWN), OWN), :]
            return 0

        lax.fori_loop(0, WIDE, one, 0)

        def two(i, _, ref=ref, to_target=to_target):
            tvol[pl.ds((to_target + i) * YP + Y0, OWN), :] = ref[pl.ds(pl.multiple_of(wide + i * OWN, OWN), OWN), :]
            return 0

        lax.fori_loop(0, NEAR, two, 0)
    even = lax.rem(lax.axis_index("gy"), 2) == 0
    for ref, after in ((cols_a, even), (cols_b, jnp.logical_not(even))):
        y = jnp.where(after, Y0 + OWN, Y0 - WIDE)
        for j in range(WIDE):
            for i in range(XB):
                vol[pl.ds(i * 8 * YP + y + j, 8, stride=YP), :] = ref[pl.ds((j * XB + i) * 8, 8), :]
        y = jnp.where(after, Y0 + OWN, Y0 - NEAR)
        for j in range(NEAR):
            for i in range(TB):
                tvol[pl.ds((NEAR + i * 8) * YP + y + j, 8, stride=YP), :] = ref[
                    pl.ds((WIDE * XB + j * TB + i) * 8, 8), :
                ]


def erode_rows(vol, k, first, count, axes):
    nb = axes.nb
    base = k * PLANE
    axes.fence(vol, base, HIGH)

    def group(i, _):
        x = first + i * RE
        v = [load(vol, base, x + j - 1, nb) for j in range(RE + 2)]
        m = [
            each(jnp.minimum, v[j], v[j - 1], v[j + 1], *axes.along_y(v[j], HIGH), *axes.along_z(v[j], HIGH))
            for j in range(1, RE + 1)
        ]
        for j in range(RE):
            store(vol, base + PLANE, x + j, nb, m[j])
        return 0

    lax.fori_loop(0, lax.div(count + RE - 1, RE), group, 0)


def skeleton_rows(vol, k, first, count, axes, skel, delta_ref):
    base = k * PLANE
    axes.fence(vol, base + PLANE, LOW)

    def group(i, _):
        x = first + i * RD
        e = [load(vol, base + PLANE, x + j - 1, 4) for j in range(RD + 2)]
        v = [load(vol, base, x + j, 4) for j in range(RD)]
        s = [load_dense(skel, k * DENSE, x + j) for j in range(RD)]
        deltas, sums = [], []
        for j in range(RD):
            a = each(jnp.maximum, e[j + 1], e[j], e[j + 2])
            b = each(jnp.maximum, a, *axes.along_y(a, LOW))
            d = each(jnp.maximum, b, *axes.along_z(b, LOW))
            delta = [jnp.maximum(p - q, 0.0) for p, q in zip(v[j], d)]
            deltas.append(delta)
            sums.append([p + jnp.maximum(q - p * q, 0.0) for p, q in zip(s[j], delta)])
        for j in range(RD):
            if delta_ref is not None:
                store_dense(delta_ref, k * DENSE, x + j, deltas[j])
            store_dense(skel, (k + 1) * DENSE, x + j, sums[j])
        return 0

    lax.fori_loop(0, (count + RD - 1) // RD, group, 0)


def forward_kernel(
    pred, target, rows_a, rows_b, cols_a, cols_b, vol, skel, delta, cot, skel_target, sums, tvol, tskel
):
    unpack(pred, target, rows_a, rows_b, cols_a, cols_b, vol, tvol)
    skel[0:DENSE, :] = jnp.zeros((DENSE, 128), jnp.float32)
    tskel[0:DENSE, :] = jnp.zeros((DENSE, 128), jnp.float32)
    five, four = Axes(5), Axes(4)
    near = WIDE - NEAR
    end = WIDE + OWN + NEAR

    def step(k, _):
        erode_rows(vol, k, 1 + k, 34 - 2 * k, five)
        erode_rows(tvol, k, near + 1 + k, 24 - 2 * k, four)
        skeleton_rows(vol, k, near, end - near, four, skel, delta)
        skeleton_rows(tvol, k, WIDE, OWN, four, tskel, None)
        return 0

    lax.fori_loop(0, ITERS + 1, step, 0)
    sub = sublanes()
    own_y = (sub >= 2) & (sub < 6)
    inside_y = jnp.logical_not(((sub < 2) & four.first_y) | ((sub >= 6) & four.last_y))
    done = (ITERS + 1) * DENSE
    zero = jnp.zeros((8, 128), jnp.float32)

    def total(x, acc):
        sp, st = load_dense(skel, done, x), load_dense(tskel, done, x)
        p, t = load(vol, 0, x, 4), load(tvol, 0, x, 4)
        a = acc[0] + sum(u * w for u, w in zip(sp, t))
        c = acc[2] + sum(u * w for u, w in zip(st, p))
        store_dense(skel_target, 0, x - WIDE, st)
        return a, acc[1] + sum(sp), c, acc[3] + sum(st)

    acc = lax.fori_loop(WIDE, WIDE + OWN, total, (zero,) * 4)
    lane = lax.broadcasted_iota(jnp.int32, (8, 128), 1)
    row = jnp.zeros((8, 128), jnp.float32)
    for i in range(4):
        row = jnp.where(lane == i, jnp.sum(jnp.where(own_y, acc[i], 0.0)), row)
    for i in range(sums.shape[0] // 8):
        sums[i * 8 : i * 8 + 8, :] = row

    def start(x, _):
        outside = ((x < WIDE) & four.first_x) | ((x >= WIDE + OWN) & four.last_x)
        keep = inside_y & jnp.logical_not(outside)
        t = load(tvol, 0, x, 4)
        store_dense(cot, 0, x, [jnp.where(keep, a, 0.0) for a in t])
        store_dense(cot, DENSE, x, [jnp.where(keep, 1.0, 0.0)] * 4)
        return 0

    lax.fori_loop(near, end, start, 0)


def split_weight(v, other, tie):
    return jnp.where(v > other, 0.0, jnp.where(v == other, tie, 1.0))


def split_weight_min(v, other, tie):
    return jnp.where(v < other, 0.0, jnp.where(v == other, tie, 1.0))


def pool_weights(v, low, up, q, minimum):
    pick, weight = (jnp.minimum, split_weight_min) if minimum else (jnp.maximum, split_weight)
    t = pick(low, v)
    to_up = weight(t, up, 0.5)
    to_low = weight(v, low, q)
    return to_low * (1.0 - to_up), to_up, pick(t, up)


def backward_kernel(vol, skel, delta, cot, grad_t, grad_1, gs, ga, gd):
    axes = Axes(4)
    near, end = WIDE - NEAR, WIDE + OWN + NEAR
    gs[...] = cot[...]
    ga[...] = jnp.zeros((2 * DENSE, 128), jnp.float32)
    zeros = [jnp.zeros((8, 128), jnp.float32)] * 4
    pair = (0, DENSE)

    def step(i, _):
        k = ITERS - i
        base = k * PLANE

        first = 8 - k

        def undilate(i, carry):
            x = first + i * RU
            rows = range(RU)
            e = [load(vol, base + PLANE, x + j - 1, 4) for j in range(RU + 2)]
            d = [load_dense(delta, k * DENSE, x + j) for j in rows]
            s = [load_dense(skel, k * DENSE, x + j) for j in rows]
            g_in = [[load_dense(gs, at, x + j) for j in rows] for at in pair]
            old = [[load_dense(ga, at, x + j - 1) for j in rows] for at in pair]
            wx = [
                [pool_weights(p, q, r, axes.q_x(x + j), False) for p, q, r in zip(e[j + 1], e[j], e[j + 2])] for j in rows
            ]
            wy, wz = [], []
            for j in rows:
                a = [w[2] for w in wx[j]]
                low, up = axes.along_y(a, LOW)
                wy.append(
                    [pool_weights(a[n], low[n], up[n], axes.q_y if n == axes.up_b else 0.5, False) for n in range(4)]
                )
                a = [w[2] for w in wy[j]]
                low, up = axes.along_z(a, LOW)
                wz.append([pool_weights(a[n], low[n], up[n], axes.q_z, False) for n in range(4)])
            out, writes = [], []
            for c, at in enumerate(pair):
                pending, ahead = carry[c]
                for j in rows:
                    g = g_in[c][j]
                    kept = [jnp.where(u - v * u > 0.0, w, 0.0) for u, v, w in zip(d[j], s[j], g)]
                    writes.append((gs, at, x + j, [w - m * u for u, m, w in zip(d[j], kept, g)]))
                    g = [jnp.where(u > 0.0, m * (1.0 - v), 0.0) for u, v, m in zip(d[j], s[j], kept)]
                    writes.append((gd, at, x + j, g))
                    for w3, back in ((wz[j], back_z), (wy[j], axes.back_y), (wx[j], None)):
                        gl, gu = [h * w[0] for h, w in zip(g, w3)], [h * w[1] for h, w in zip(g, w3)]
                        g = [h - m - n for h, m, n in zip(g, gl, gu)]
                        if back is not None:
                            g = each(jnp.add, g, back(gl, gu))
                    writes.append((ga, at, x + j - 1, [h - m - n for h, m, n in zip(old[c][j], pending, gl)]))
                    pending, ahead = each(jnp.add, g, ahead), gu
                out.append((pending, ahead))
            for ref, at, row, v in writes:
                store_dense(ref, at, row, v)
            return out

        axes.fence(vol, base + PLANE, LOW)
        lax.fori_loop(0, lax.div(20 + 2 * k + RU - 1, RU), undilate, [(zeros, zeros)] * 2)
        start = 9 - k

        def unerode(i, carry):
            x = start + i * RV
            rows = range(RV)
            v = [load(vol, base, x + j - 1, 4) for j in range(RV + 2)]
            g_in = [[load_dense(ga, at, x + j) for j in rows] for at in pair]
            direct = [[load_dense(gd, at, x + j - 1) for j in rows] for at in pair]
            shares = []
            for j in rows:
                wx = [pool_weights(p, q, r, axes.q_x(x + j), True) for p, q, r in zip(v[j + 1], v[j], v[j + 2])]
                low, up = axes.along_y(v[j + 1], HIGH)
                wy = [
                    pool_weights(v[j + 1][n], low[n], up[n], axes.q_y if n == axes.up_b else 0.5, True)
                    for n in range(4)
                ]
                low, up = axes.along_z(v[j + 1], HIGH)
                wz = [pool_weights(v[j + 1][n], low[n], up[n], axes.q_z, True) for n in range(4)]
                share = []
                for n in range(4):
                    one, two, three = wx[n][2], wy[n][2], wz[n][2]
                    to_three = split_weight_min(jnp.minimum(one, two), three, 0.5)
                    rest = 1.0 - to_three
                    to_two = split_weight_min(one, two, 0.5) * rest
                    to_one = rest - to_two
                    share.append(
                        (to_one * wx[n][0], to_one * wx[n][1], to_two * wy[n][0], to_two * wy[n][1],
                         to_three * wz[n][0], to_three * wz[n][1])
                    )
                shares.append(share)
            out, writes = [], []
            for c, at in enumerate(pair):
                pending, ahead = carry[c]
                for j in rows:
                    g = g_in[c][j]
                    parts = [[h * w[n] for h, w in zip(g, shares[j])] for n in range(6)]
                    for part in parts:
                        g = [h - m for h, m in zip(g, part)]
                    g = each(jnp.add, g, axes.back_y(parts[2], parts[3]), back_z(parts[4], parts[5]), ahead)
                    writes.append((ga, at, x + j - 1, each(jnp.add, direct[c][j], pending, parts[0])))
                    pending, ahead = g, parts[1]
                out.append((pending, ahead))
            for ref, at, row, v in writes:
                store_dense(ref, at, row, v)
            return out

        axes.fence(vol, base, HIGH)
        lax.fori_loop(0, lax.div(18 + 2 * k + RV - 1, RV), unerode, [(zeros, zeros)] * 2)
        return 0

    lax.fori_loop(0, ITERS + 1, step, 0)
    own = pl.ds(WIDE * LV, OWN * LV)
    grad_t[...] = ga[own, :]
    grad_1[...] = ga[pl.ds(DENSE + WIDE * LV, OWN * LV), :]


def finish_kernel(cells, sums, grad_t, grad_1, skel_target, gradient, loss, natural):
    total = jnp.zeros((8, 128), jnp.float32)
    for i in range(sums.shape[0] // 8):
        total = total + sums[i * 8 : i * 8 + 8, :]
    lane = lanes()
    sum_a, sum_b, sum_c, sum_d = (
        jnp.broadcast_to(jnp.sum(jnp.where(lane == i, total, 0.0)), (8, 128)) for i in range(4)
    )
    precision = (sum_a + 1.0) / (sum_b + 1.0)
    sensitivity = (sum_c + 1.0) / (sum_d + 1.0)
    together = precision + sensitivity
    loss[...] = 1.0 - 2.0 * precision * sensitivity / together
    coef_pred = cells * (-2.0 * sensitivity * sensitivity / (together * together)) / (sum_b + 1.0)
    coef_target = cells * (-2.0 * precision * precision / (together * together)) / (sum_d + 1.0)

    def row(x, _):
        t, one, s = load_dense(grad_t, 0, x), load_dense(grad_1, 0, x), load_dense(skel_target, 0, x)
        for b in range(4):
            natural[pl.ds(x * LV + b, 8, stride=4), :] = (
                coef_pred * (t[b] - precision * one[b]) + coef_target * s[b]
            )
        return 0

    lax.fori_loop(0, OWN, row, 0)
    for x in range(OWN):
        gradient[x * OWN : (x + 1) * OWN, :] = natural[x * LV + 8 : x * LV + 24, :]


def call(kernel, out, scratch=(), cost=None):
    vmem = pl.BlockSpec(memory_space=pltpu.VMEM)

    def run(*args):
        return pl.pallas_call(
            kernel,
            out_shape=[jax.ShapeDtypeStruct(s, jnp.float32) for s in out],
            in_specs=[vmem] * len(args),
            out_specs=[vmem] * len(out),
            scratch_shapes=[pltpu.VMEM(s, jnp.float32) for s in scratch],
            compiler_params=pltpu.CompilerParams(vmem_limit_bytes=12 * 2**20),
            cost_estimate=cost,
        )(*args)

    return run


def swapped(value, axis, shift):
    size = lax.axis_size(axis)
    pairs = [((i + shift) % size, ((i ^ 1) + shift) % size) for i in range(size)]
    return lax.ppermute(value, axis, pairs)


def body(prediction, label_mask, confidence):
    rows, cols, planes = prediction.shape
    flat = (rows * cols, planes)
    devices = lax.axis_size("gx") * lax.axis_size("gy")
    cells = float(devices * rows * cols * planes)
    pred = prediction.reshape(flat)
    side = ((WIDE + NEAR) * OWN, 128)
    target, send_a, send_b = call(pack_rows_kernel, [flat, side, side])(
        pred, label_mask.reshape(flat), confidence.reshape(flat)
    )
    rows_a, rows_b = swapped(send_a, "gx", 0), swapped(send_b, "gx", 1)
    side = (SEND, 128)
    send_a, send_b = call(
        pack_columns_kernel, [side, side], [(XB * 8 * OWN, 128), (TB * 8 * OWN, 128)]
    )(pred, target, rows_a, rows_b)
    cols_a, cols_b = swapped(send_a, "gy", 0), swapped(send_b, "gy", 1)
    levels = ITERS + 2
    vol, skel, delta, cot, skel_target, sums = call(
        forward_kernel,
        [(levels * PLANE, 128), (levels * DENSE, 128), ((ITERS + 1) * DENSE, 128), (2 * DENSE, 128), (OWN * LV, 128), (devices, 128)],
        [(levels * PLANE, 128), (levels * DENSE, 128)],
    )(pred, target, rows_a, rows_b, cols_a, cols_b)
    sums = lax.all_to_all(sums.reshape(devices, 1, 128), ("gx", "gy"), 0, 0).reshape(devices, 128)
    grad_t, grad_1 = call(
        backward_kernel,
        [(OWN * LV, 128)] * 2,
        [(2 * DENSE, 128)] * 3,
        pl.CostEstimate(flops=100_000_000, bytes_accessed=20_000_000, transcendentals=0),
    )(vol, skel, delta, cot)

    def finish(*refs):
        finish_kernel(jnp.float32(cells), *refs)

    gradient, loss = call(finish, [flat, (8, 128)], [(OWN * LV, 128)])(sums, grad_t, grad_1, skel_target)
    return gradient.reshape(rows, cols, planes), loss[0, 0]


def solution(mesh):
    placed = (P("gx", "gy", None), P("gx", "gy", None), P("gx", "gy", None))
    return jax.shard_map(
        body, mesh=mesh, in_specs=placed, out_specs=(P("gx", "gy", None), P()), check_vma=False
    )
```

```python
import jax
import jax.numpy as jnp
from jax import lax
from jax.experimental import pallas as pl
from jax.experimental.pallas import tpu as pltpu
from jax.sharding import PartitionSpec as P

ITERS = 3
RE, RD, RT, RU, RV = 9, 7, 8, 5, 6
OWN = 16
WIDE = 10
NEAR = 5
YP = 40
Y0 = 12
XP = 40
HIGH, LOW = 2.0, -1.0
PLANE = XP * YP
LV = 32
DENSE = XP * LV


def lanes():
    return lax.broadcasted_iota(jnp.int32, (8, 128), 1)


def sublanes():
    return lax.broadcasted_iota(jnp.int32, (8, 128), 0)


class Axes:
    def __init__(self, nb):
        size_x, size_y = lax.axis_size("gx"), lax.axis_size("gy")
        gx, gy = lax.axis_index("gx"), lax.axis_index("gy")
        self.first_x, self.last_x = gx == 0, gx == size_x - 1
        self.first_y, self.last_y = gy == 0, gy == size_y - 1
        self.nb = nb
        start = 0 if nb == 5 else 4
        self.low_s, self.low_b = divmod(Y0 - start, nb)
        self.up_s, self.up_b = divmod(Y0 + OWN - 1 - start, nb)
        sub, lane = sublanes(), lanes()
        self.low_y = (sub == self.low_s) & self.first_y
        self.up_y = (sub == self.up_s) & self.last_y
        self.low_z, self.up_z = lane == 0, lane == 127
        self.q_y = jnp.where(self.up_y, 0.25, 0.5)
        self.q_z = jnp.where(self.up_z, 0.25, 0.5)

    def fence(self, ref, base, value):
        for face, x in ((self.first_x, WIDE - 1), (self.last_x, WIDE + OWN)):

            @pl.when(face)
            def _(x=x):
                ref[pl.ds(pl.multiple_of(base + x * YP, 8), YP), :] = jnp.full((YP, 128), value, jnp.float32)

    def q_x(self, x):
        return jnp.where((x == WIDE + OWN - 1) & self.last_x, 0.25, 0.5)

    def along_y(self, v, fill):
        nb = self.nb
        lower = [pltpu.roll(v[nb - 1], 1, 0)] + v[: nb - 1]
        upper = v[1:] + [pltpu.roll(v[0], 7, 0)]
        lower[self.low_b] = jnp.where(self.low_y, fill, lower[self.low_b])
        upper[self.up_b] = jnp.where(self.up_y, fill, upper[self.up_b])
        return lower, upper

    def along_z(self, v, fill):
        lower = [jnp.where(self.low_z, fill, pltpu.roll(a, 1, 1)) for a in v]
        upper = [jnp.where(self.up_z, fill, pltpu.roll(a, 127, 1)) for a in v]
        return lower, upper

    def back_y(self, gl, gu):
        nb = self.nb
        from_above = gl[1:] + [pltpu.roll(gl[0], 7, 0)]
        from_below = [pltpu.roll(gu[nb - 1], 1, 0)] + gu[: nb - 1]
        return [a + b for a, b in zip(from_above, from_below)]


def back_z(gl, gu):
    return [pltpu.roll(a, 127, 1) + pltpu.roll(b, 1, 1) for a, b in zip(gl, gu)]


def load(ref, base, x, nb):
    start = 0 if nb == 5 else 4
    return [ref[pl.ds(base + x * YP + start + b, 8, stride=nb), :] for b in range(nb)]


def store(ref, base, x, nb, v):
    start = 0 if nb == 5 else 4
    for b in range(nb):
        ref[pl.ds(base + x * YP + start + b, 8, stride=nb), :] = v[b]


def load_dense(ref, base, x):
    return [ref[pl.ds(pl.multiple_of(base + x * LV + 8 * b, 8), 8), :] for b in range(4)]


def store_dense(ref, base, x, v):
    for b in range(4):
        ref[pl.ds(pl.multiple_of(base + x * LV + 8 * b, 8), 8), :] = v[b]


def inside_columns(axes):
    sub = sublanes()
    return jnp.logical_not(((sub < 2) & axes.first_y) | ((sub >= 6) & axes.last_y))


def inside_row(x, axes):
    return jnp.logical_not(((x < WIDE) & axes.first_x) | ((x >= WIDE + OWN) & axes.last_x))


def each(pick, *lists):
    out = lists[0]
    for other in lists[1:]:
        out = [pick(a, b) for a, b in zip(out, other)]
    return out


def pack_rows_kernel(pred_in, label_in, conf_in, pred, target, send_a, send_b, label, conf, sems):
    copies = [
        pltpu.make_async_copy(src, dst, sems.at[i])
        for i, (src, dst) in enumerate(((pred_in, pred), (label_in, label), (conf_in, conf)))
    ]
    for copy in copies:
        copy.start()
    for copy in copies:
        copy.wait()
    even = lax.rem(lax.axis_index("gx"), 2) == 0
    target[...] = label[...].astype(jnp.float32) * conf[...]
    wide, near = WIDE * OWN, NEAR * OWN
    total = OWN * OWN
    for ref, last in ((send_a, even), (send_b, jnp.logical_not(even))):
        from_pred = pl.multiple_of(jnp.where(last, total - wide, 0), 8)
        from_target = pl.multiple_of(jnp.where(last, total - near, 0), 8)
        ref[0:wide, :] = pred[pl.ds(from_pred, wide), :]
        ref[wide : wide + near, :] = target[pl.ds(from_target, near), :]


XB, TB = 5, 4
SEND = (WIDE * XB + NEAR * TB) * 8


def pack_columns_kernel(pred, target, rows_a, rows_b, send_a, send_b, wide_pred, wide_target):
    even = lax.rem(lax.axis_index("gx"), 2) == 0
    wide, near, total = WIDE * OWN, NEAR * OWN, OWN * OWN
    wide_pred[wide : wide + total, :] = pred[...]
    wide_target[near : near + total, :] = target[...]
    for ref, after in ((rows_a, even), (rows_b, jnp.logical_not(even))):
        to_pred = pl.multiple_of(jnp.where(after, wide + total, 0), 8)
        to_target = pl.multiple_of(jnp.where(after, near + total, 0), 8)
        wide_pred[pl.ds(to_pred, wide), :] = ref[0:wide, :]
        wide_target[pl.ds(to_target, near), :] = ref[wide : wide + near, :]
    even = lax.rem(lax.axis_index("gy"), 2) == 0
    for ref, last in ((send_a, even), (send_b, jnp.logical_not(even))):
        start = jnp.where(last, OWN - WIDE, 0)
        for j in range(WIDE):
            for i in range(XB):
                ref[pl.ds((j * XB + i) * 8, 8), :] = wide_pred[pl.ds(i * 128 + start + j, 8, stride=OWN), :]
        start = jnp.where(last, OWN - NEAR, 0)
        for j in range(NEAR):
            for i in range(TB):
                ref[pl.ds((WIDE * XB + j * TB + i) * 8, 8), :] = wide_target[
                    pl.ds(i * 128 + start + j, 8, stride=OWN), :
                ]


def unpack(pred, target, rows_a, rows_b, cols_a, cols_b, vol, tvol):
    even = lax.rem(lax.axis_index("gx"), 2) == 0
    wide = WIDE * OWN

    def whole(i, _):
        own = pl.ds(pl.multiple_of(i * OWN, OWN), OWN)
        vol[pl.ds((WIDE + i) * YP + Y0, OWN), :] = pred[own, :]
        tvol[pl.ds((WIDE + i) * YP + Y0, OWN), :] = target[own, :]
        return 0

    lax.fori_loop(0, OWN, whole, 0)
    for ref, after in ((rows_a, even), (rows_b, jnp.logical_not(even))):
        to_pred = jnp.where(after, WIDE + OWN, 0)
        to_target = jnp.where(after, WIDE + OWN, WIDE - NEAR)

        def one(i, _, ref=ref, to_pred=to_pred):
            vol[pl.ds((to_pred + i) * YP + Y0, OWN), :] = ref[pl.ds(pl.multiple_of(i * OWN, OWN), OWN), :]
            return 0

        lax.fori_loop(0, WIDE, one, 0)

        def two(i, _, ref=ref, to_target=to_target):
            tvol[pl.ds((to_target + i) * YP + Y0, OWN), :] = ref[pl.ds(pl.multiple_of(wide + i * OWN, OWN), OWN), :]
            return 0

        lax.fori_loop(0, NEAR, two, 0)
    even = lax.rem(lax.axis_index("gy"), 2) == 0
    for ref, after in ((cols_a, even), (cols_b, jnp.logical_not(even))):
        y = jnp.where(after, Y0 + OWN, Y0 - WIDE)
        for j in range(WIDE):
            for i in range(XB):
                vol[pl.ds(i * 8 * YP + y + j, 8, stride=YP), :] = ref[pl.ds((j * XB + i) * 8, 8), :]
        y = jnp.where(after, Y0 + OWN, Y0 - NEAR)
        for j in range(NEAR):
            for i in range(TB):
                tvol[pl.ds((NEAR + i * 8) * YP + y + j, 8, stride=YP), :] = ref[
                    pl.ds((WIDE * XB + j * TB + i) * 8, 8), :
                ]


def erode_rows(vol, k, first, count, axes):
    nb = axes.nb
    base = k * PLANE
    axes.fence(vol, base, HIGH)

    def group(i, _):
        x = first + i * RE
        v = [load(vol, base, x + j - 1, nb) for j in range(RE + 2)]
        m = [
            each(jnp.minimum, v[j], v[j - 1], v[j + 1], *axes.along_y(v[j], HIGH), *axes.along_z(v[j], HIGH))
            for j in range(1, RE + 1)
        ]
        for j in range(RE):
            store(vol, base + PLANE, x + j, nb, m[j])
        return 0

    lax.fori_loop(0, lax.div(count + RE - 1, RE), group, 0)


def skeleton_rows(vol, k, first, count, axes, skel, delta_ref, take):
    base = k * PLANE
    axes.fence(vol, base + PLANE, LOW)

    def group(i, _):
        x = first + i * take
        e = [load(vol, base + PLANE, x + j - 1, 4) for j in range(take + 2)]
        v = [load(vol, base, x + j, 4) for j in range(take)]
        s = [load_dense(skel, k * DENSE, x + j) for j in range(take)]
        deltas, sums = [], []
        for j in range(take):
            a = each(jnp.maximum, e[j + 1], e[j], e[j + 2])
            b = each(jnp.maximum, a, *axes.along_y(a, LOW))
            d = each(jnp.maximum, b, *axes.along_z(b, LOW))
            delta = [jnp.maximum(p - q, 0.0) for p, q in zip(v[j], d)]
            deltas.append(delta)
            sums.append([p + jnp.maximum(q - p * q, 0.0) for p, q in zip(s[j], delta)])
        for j in range(take):
            if delta_ref is not None:
                store_dense(delta_ref, k * DENSE, x + j, deltas[j])
            store_dense(skel, (k + 1) * DENSE, x + j, sums[j])
        return 0

    lax.fori_loop(0, (count + take - 1) // take, group, 0)


KEPT, SAVED = 30, 28
FROM, START = 4, WIDE - NEAR


def kept(ref, at, plane=0, packed=False):
    if packed:
        return ref.at[pl.ds(plane * KEPT * YP, KEPT * YP), :]
    return ref.at[pl.ds(at + FROM * YP, KEPT * YP), :]


def saved(ref, at, plane=0, packed=False):
    if packed:
        return ref.at[pl.ds(plane * SAVED * LV, SAVED * LV), :]
    return ref.at[pl.ds(at + START * LV, SAVED * LV), :]


def state(vol, skel, delta, cot, far):
    vol_h, skel_h, delta_h, cot_h = far
    levels = ITERS + 1
    pairs = [(saved(cot, 0), saved(cot_h, 0, 0, True)), (kept(vol, levels * PLANE), kept(vol_h, 0, levels, True))]
    for k in range(ITERS, -1, -1):
        pairs.append((saved(delta, k * DENSE), saved(delta_h, 0, k, True)))
        pairs.append((kept(vol, k * PLANE), kept(vol_h, 0, k, True)))
        if k:
            pairs.append((saved(skel, k * DENSE), saved(skel_h, 0, k - 1, True)))
    return pairs


COPIES = 2 + 3 * (ITERS + 1) - 1


def forward_kernel(
    pred, target, rows_a, rows_b, cols_a, cols_b, vol_h, skel_h, delta_h, cot_h, skel_target, sums,
    vol, skel, delta, cot, tvol, tskel, sems,
):
    unpack(pred, target, rows_a, rows_b, cols_a, cols_b, vol, tvol)
    skel[0:DENSE, :] = jnp.zeros((DENSE, 128), jnp.float32)
    tskel[0:DENSE, :] = jnp.zeros((DENSE, 128), jnp.float32)
    five, four = Axes(5), Axes(4)
    near = WIDE - NEAR
    end = WIDE + OWN + NEAR
    masks = inside_columns(four)

    def start(x, _):
        keep = masks & inside_row(x, four)
        store_dense(cot, 0, x, [jnp.where(keep, a, 0.0) for a in load(tvol, 0, x, 4)])
        return 0

    lax.fori_loop(near, end, start, 0)

    def step(k, _):
        erode_rows(vol, k, 1 + k, 34 - 2 * k, five)
        skeleton_rows(vol, k, near, end - near, four, skel, delta, RD)
        return 0

    lax.fori_loop(0, ITERS + 1, step, 0)
    copies = [
        pltpu.make_async_copy(src, dst, sems.at[i])
        for i, (src, dst) in enumerate(state(vol, skel, delta, cot, (vol_h, skel_h, delta_h, cot_h)))
    ]
    for copy in copies:
        copy.start()

    def step(k, _):
        erode_rows(tvol, k, near + 1 + k, 24 - 2 * k, four)
        skeleton_rows(tvol, k, WIDE, OWN, four, tskel, None, RT)
        return 0

    lax.fori_loop(0, ITERS + 1, step, 0)
    done = (ITERS + 1) * DENSE
    copies.append(
        pltpu.make_async_copy(tskel.at[pl.ds(done + WIDE * LV, OWN * LV), :], skel_target, sems.at[COPIES])
    )
    copies[-1].start()
    sub = sublanes()
    own_y = (sub >= 2) & (sub < 6)
    zero = jnp.zeros((8, 128), jnp.float32)

    def total(x, acc):
        sp, st = load_dense(skel, done, x), load_dense(tskel, done, x)
        p, t = load(vol, 0, x, 4), load(tvol, 0, x, 4)
        a = acc[0] + sum(u * w for u, w in zip(sp, t))
        c = acc[2] + sum(u * w for u, w in zip(st, p))
        return a, acc[1] + sum(sp), c, acc[3] + sum(st)

    acc = lax.fori_loop(WIDE, WIDE + OWN, total, (zero,) * 4)
    lane = lax.broadcasted_iota(jnp.int32, (8, 128), 1)
    row = jnp.zeros((8, 128), jnp.float32)
    for i in range(4):
        row = jnp.where(lane == i, jnp.sum(jnp.where(own_y, acc[i], 0.0)), row)
    for i in range(sums.shape[0] // 8):
        sums[i * 8 : i * 8 + 8, :] = row

    for copy in copies:
        copy.wait()


def split_weight(v, other, tie):
    return jnp.where(v > other, 0.0, jnp.where(v == other, tie, 1.0))


def split_weight_min(v, other, tie):
    return jnp.where(v < other, 0.0, jnp.where(v == other, tie, 1.0))


def pool_weights(v, low, up, q, minimum):
    pick, weight = (jnp.minimum, split_weight_min) if minimum else (jnp.maximum, split_weight)
    t = pick(low, v)
    to_up = weight(t, up, 0.5)
    to_low = weight(v, low, q)
    return to_low * (1.0 - to_up), to_up, pick(t, up)


def backward_kernel(vol_h, skel_h, delta_h, cot_h, grad_t, grad_1, vol, skel, delta, gs, ga, gd, sems):
    copies = [
        pltpu.make_async_copy(src, dst, sems.at[i])
        for i, (dst, src) in enumerate(state(vol, skel, delta, gs, (vol_h, skel_h, delta_h, cot_h)))
    ]
    for copy in copies:
        copy.start()
    axes = Axes(4)
    near, end = WIDE - NEAR, WIDE + OWN + NEAR
    ga[...] = jnp.zeros((2 * DENSE, 128), jnp.float32)
    skel[0:DENSE, :] = jnp.zeros((DENSE, 128), jnp.float32)
    masks = inside_columns(axes)

    def ones(x, _):
        store_dense(gs, DENSE, x, [jnp.where(masks & inside_row(x, axes), 1.0, 0.0)] * 4)
        return 0

    lax.fori_loop(near, end + 2, ones, 0)
    zeros = [jnp.zeros((8, 128), jnp.float32)] * 4
    pair = (0, DENSE)
    for copy in copies:
        copy.wait()

    def step(i, _):
        k = ITERS - i
        base = k * PLANE

        first = 8 - k

        def undilate(i, carry):
            x = first + i * RU
            rows = range(RU)
            e = [load(vol, base + PLANE, x + j - 1, 4) for j in range(RU + 2)]
            d = [load_dense(delta, k * DENSE, x + j) for j in rows]
            s = [load_dense(skel, k * DENSE, x + j) for j in rows]
            g_in = [[load_dense(gs, at, x + j) for j in rows] for at in pair]
            old = [[load_dense(ga, at, x + j - 1) for j in rows] for at in pair]
            wx = [
                [pool_weights(p, q, r, axes.q_x(x + j), False) for p, q, r in zip(e[j + 1], e[j], e[j + 2])] for j in rows
            ]
            wy, wz = [], []
            for j in rows:
                a = [w[2] for w in wx[j]]
                low, up = axes.along_y(a, LOW)
                wy.append(
                    [pool_weights(a[n], low[n], up[n], axes.q_y if n == axes.up_b else 0.5, False) for n in range(4)]
                )
                a = [w[2] for w in wy[j]]
                low, up = axes.along_z(a, LOW)
                wz.append([pool_weights(a[n], low[n], up[n], axes.q_z, False) for n in range(4)])
            out, writes = [], []
            for c, at in enumerate(pair):
                pending, ahead = carry[c]
                for j in rows:
                    g = g_in[c][j]
                    kept = [jnp.where(u - v * u > 0.0, w, 0.0) for u, v, w in zip(d[j], s[j], g)]
                    writes.append((gs, at, x + j, [w - m * u for u, m, w in zip(d[j], kept, g)]))
                    g = [jnp.where(u > 0.0, m * (1.0 - v), 0.0) for u, v, m in zip(d[j], s[j], kept)]
                    writes.append((gd, at, x + j, g))
                    for w3, back in ((wz[j], back_z), (wy[j], axes.back_y), (wx[j], None)):
                        gl, gu = [h * w[0] for h, w in zip(g, w3)], [h * w[1] for h, w in zip(g, w3)]
                        g = [h - m - n for h, m, n in zip(g, gl, gu)]
                        if back is not None:
                            g = each(jnp.add, g, back(gl, gu))
                    writes.append((ga, at, x + j - 1, [h - m - n for h, m, n in zip(old[c][j], pending, gl)]))
                    pending, ahead = each(jnp.add, g, ahead), gu
                out.append((pending, ahead))
            for ref, at, row, v in writes:
                store_dense(ref, at, row, v)
            return out

        axes.fence(vol, base + PLANE, LOW)
        lax.fori_loop(0, lax.div(20 + 2 * k + RU - 1, RU), undilate, [(zeros, zeros)] * 2)
        start = 9 - k

        def unerode(i, carry):
            x = start + i * RV
            rows = range(RV)
            v = [load(vol, base, x + j - 1, 4) for j in range(RV + 2)]
            g_in = [[load_dense(ga, at, x + j) for j in rows] for at in pair]
            direct = [[load_dense(gd, at, x + j - 1) for j in rows] for at in pair]
            shares = []
            for j in rows:
                wx = [pool_weights(p, q, r, axes.q_x(x + j), True) for p, q, r in zip(v[j + 1], v[j], v[j + 2])]
                low, up = axes.along_y(v[j + 1], HIGH)
                wy = [
                    pool_weights(v[j + 1][n], low[n], up[n], axes.q_y if n == axes.up_b else 0.5, True)
                    for n in range(4)
                ]
                low, up = axes.along_z(v[j + 1], HIGH)
                wz = [pool_weights(v[j + 1][n], low[n], up[n], axes.q_z, True) for n in range(4)]
                share = []
                for n in range(4):
                    one, two, three = wx[n][2], wy[n][2], wz[n][2]
                    to_three = split_weight_min(jnp.minimum(one, two), three, 0.5)
                    rest = 1.0 - to_three
                    to_two = split_weight_min(one, two, 0.5) * rest
                    to_one = rest - to_two
                    share.append(
                        (to_one * wx[n][0], to_one * wx[n][1], to_two * wy[n][0], to_two * wy[n][1],
                         to_three * wz[n][0], to_three * wz[n][1])
                    )
                shares.append(share)
            out, writes = [], []
            for c, at in enumerate(pair):
                pending, ahead = carry[c]
                for j in rows:
                    g = g_in[c][j]
                    parts = [[h * w[n] for h, w in zip(g, shares[j])] for n in range(6)]
                    for part in parts:
                        g = [h - m for h, m in zip(g, part)]
                    g = each(jnp.add, g, axes.back_y(parts[2], parts[3]), back_z(parts[4], parts[5]), ahead)
                    writes.append((ga, at, x + j - 1, each(jnp.add, direct[c][j], pending, parts[0])))
                    pending, ahead = g, parts[1]
                out.append((pending, ahead))
            for ref, at, row, v in writes:
                store_dense(ref, at, row, v)
            return out

        axes.fence(vol, base, HIGH)
        lax.fori_loop(0, lax.div(18 + 2 * k + RV - 1, RV), unerode, [(zeros, zeros)] * 2)
        return 0

    lax.fori_loop(0, ITERS + 1, step, 0)
    copies = [
        pltpu.make_async_copy(ga.at[pl.ds(at + WIDE * LV, OWN * LV), :], out, sems.at[i])
        for i, (at, out) in enumerate(((0, grad_t), (DENSE, grad_1)))
    ]
    for copy in copies:
        copy.start()
    for copy in copies:
        copy.wait()


def finish_kernel(cells, sums, far_t, far_1, far_skel, gradient, loss, natural, grad_t, grad_1, skel_target, sems):
    copies = [
        pltpu.make_async_copy(src, dst, sems.at[i])
        for i, (src, dst) in enumerate(((far_t, grad_t), (far_1, grad_1), (far_skel, skel_target)))
    ]
    for copy in copies:
        copy.start()
    total = jnp.zeros((8, 128), jnp.float32)
    for i in range(sums.shape[0] // 8):
        total = total + sums[i * 8 : i * 8 + 8, :]
    lane = lanes()
    sum_a, sum_b, sum_c, sum_d = (
        jnp.broadcast_to(jnp.sum(jnp.where(lane == i, total, 0.0)), (8, 128)) for i in range(4)
    )
    precision = (sum_a + 1.0) / (sum_b + 1.0)
    sensitivity = (sum_c + 1.0) / (sum_d + 1.0)
    together = precision + sensitivity
    loss[...] = (1.0 - 2.0 * precision * sensitivity / together)[0:1, 0:1]
    coef_pred = cells * (-2.0 * sensitivity * sensitivity / (together * together)) / (sum_b + 1.0)
    coef_target = cells * (-2.0 * precision * precision / (together * together)) / (sum_d + 1.0)
    for copy in copies:
        copy.wait()

    def row(x, _):
        t, one, s = load_dense(grad_t, 0, x), load_dense(grad_1, 0, x), load_dense(skel_target, 0, x)
        for b in range(4):
            natural[pl.ds(x * LV + b, 8, stride=4), :] = (
                coef_pred * (t[b] - precision * one[b]) + coef_target * s[b]
            )
        return 0

    lax.fori_loop(0, OWN, row, 0)
    for x in range(OWN):
        gradient[x * OWN : (x + 1) * OWN, :] = natural[x * LV + 8 : x * LV + 24, :]


def call(kernel, out, scratch=(), cost=None, copies=0, far_in=(), far_out=()):
    near, far = pl.BlockSpec(memory_space=pltpu.VMEM), pl.BlockSpec(memory_space=pltpu.HBM)
    scratch = [pltpu.VMEM(s, d) for s, d in ((s, jnp.float32) if isinstance(s[0], int) else s for s in scratch)]
    if copies:
        scratch.append(pltpu.SemaphoreType.DMA((copies,)))

    def run(*args):
        args = [pltpu.with_memory_space_constraint(a, pltpu.HBM) if i in far_in else a for i, a in enumerate(args)]
        return pl.pallas_call(
            kernel,
            out_shape=[
                (pltpu.HBM if i in far_out else jax.ShapeDtypeStruct)(s, jnp.float32) for i, s in enumerate(out)
            ],
            in_specs=[far if i in far_in else near for i in range(len(args))],
            out_specs=[far if i in far_out else near for i in range(len(out))],
            scratch_shapes=scratch,
            compiler_params=pltpu.CompilerParams(vmem_limit_bytes=32 * 2**20),
            cost_estimate=cost,
        )(*args)

    return run


def swapped(value, axis, shift):
    size = lax.axis_size(axis)
    pairs = [((i + shift) % size, ((i ^ 1) + shift) % size) for i in range(size)]
    return lax.ppermute(value, axis, pairs)


def body(prediction, label_mask, confidence):
    rows, cols, planes = prediction.shape
    flat = (rows * cols, planes)
    devices = lax.axis_size("gx") * lax.axis_size("gy")
    cells = float(devices * rows * cols * planes)
    side = ((WIDE + NEAR) * OWN, 128)
    pred, target, send_a, send_b = call(
        pack_rows_kernel, [flat, flat, side, side], [(flat, jnp.int32), flat], copies=3, far_in=(0, 1, 2)
    )(prediction.reshape(flat), label_mask.reshape(flat), confidence.reshape(flat))
    rows_a, rows_b = swapped(send_a, "gx", 0), swapped(send_b, "gx", 1)
    side = (SEND, 128)
    send_a, send_b = call(
        pack_columns_kernel, [side, side], [(XB * 8 * OWN, 128), (TB * 8 * OWN, 128)]
    )(pred, target, rows_a, rows_b)
    cols_a, cols_b = swapped(send_a, "gy", 0), swapped(send_b, "gy", 1)
    levels = ITERS + 2
    own, saved_rows = (OWN * LV, 128), SAVED * LV
    vols, dense = (levels * PLANE, 128), (levels * DENSE, 128)
    *far, skel_target, sums = call(
        forward_kernel,
        [
            (levels * KEPT * YP, 128), (ITERS * saved_rows, 128), ((ITERS + 1) * saved_rows, 128), (saved_rows, 128),
            own, (devices, 128),
        ],
        [vols, dense, dense, (DENSE, 128), vols, dense],
        copies=COPIES + 1,
        far_out=(0, 1, 2, 3, 4),
    )(pred, target, rows_a, rows_b, cols_a, cols_b)
    sums = lax.all_to_all(sums.reshape(devices, 1, 128), ("gx", "gy"), 0, 0).reshape(devices, 128)
    grad_t, grad_1 = call(
        backward_kernel,
        [own, own],
        [vols, dense, dense] + [(2 * DENSE, 128)] * 3,
        pl.CostEstimate(flops=100_000_000, bytes_accessed=20_000_000, transcendentals=0),
        copies=COPIES,
        far_in=(0, 1, 2, 3),
        far_out=(0, 1),
    )(*far)

    def finish(*refs):
        finish_kernel(jnp.float32(cells), *refs)

    gradient, loss = call(finish, [flat, (1, 1)], [own] * 4, copies=3, far_in=(1, 2, 3))(
        sums, grad_t, grad_1, skel_target
    )
    return gradient.reshape(rows, cols, planes), loss.reshape(())


def solution(mesh):
    placed = (P("gx", "gy", None), P("gx", "gy", None), P("gx", "gy", None))
    return jax.shard_map(
        body, mesh=mesh, in_specs=placed, out_specs=(P("gx", "gy", None), P()), check_vma=False
    )
```
